256 devices in a mesh: dom: 32 (over x, y, core), mem: 8 (over z).
Axes of the slice: x: 4, y: 4, z: 8, core: 2. Of those that a mesh axis runs over, the one named last changes fastest.
Arguments:
- ensemble: bfloat16 [160, 64, 64, 128], P('mem', 'dom'), may hold values from -6 to 6
- obs_values: float32 [64, 64, 128], P('dom', 'mem'), may hold values from -9 to 9
- obs_var: float32 [64, 64, 128], P('dom', 'mem'), may hold values from 0.25 to 4
- obs_cols: int32 [64, 64, 128], P('dom', 'mem'), may hold values from 0 to 127
- obs_counts: int32 [64, 64], P('dom', 'mem'), may hold values from 16 to 128
- pattern: int32 [64, 64, 8], P(None, 'mem'), may hold values from 0 to 63, as said below
Outputs:
- analysis: bfloat16 [160, 64, 64, 128], P('mem', 'dom')
The draws below stay inside these ranges and needn't reach their ends.
Inputs may be any that keep to these rules, and one draw needn't show every extreme that they name: `pattern`: the 8 target columns of a batch are distinct; the first is the batch's own column, and the others lie on distinct indices of dom other than the batch's own. At one level group, at most 1 batch of one index of dom act on columns of any one other index, and some index pair reaches 1.
All inputs are finite; a program needn't handle non-finite values.
Results may differ from the reference program's by a relative error of at most 0.0085.
Values may be sent and summed in bfloat16 or wider, within the bound.
A program may use at most 128 MiB of HBM per device.

```python
import math
import jax
import jax.numpy as jnp
from jax import lax

K = 160
BS = 128
OB = 128
P_SIZE = 8
COL_DEV = 2
NCOL = 64
LEV = 64


def draw_obs_counts(key, part):
    key = jax.random.fold_in(key, 5)
    first, second, third = jax.random.split(key, 3)
    batches = NCOL * LEV
    counts = jax.random.randint(first, (batches,), OB // 8, OB + 1)
    fullest = jax.random.randint(second, (), 0, batches)
    sparsest = (fullest + 1 + jax.random.randint(third, (), 0, batches - 1)) % batches
    counts = counts.at[fullest].set(OB).at[sparsest].set(OB // 8)
    return counts.reshape((NCOL, LEV)).astype(jnp.int32)


def draw_pattern(key, part):
    key = jax.random.fold_in(key, 9)
    key_scores, key_within = jax.random.split(key)
    groups = NCOL // COL_DEV
    others = groups - 1
    scores = jax.random.randint(key_scores, (groups, LEV, others), 0, 1 << 20) * others + jnp.arange(others, dtype=jnp.int32)
    ordering = lax.top_k(scores, others)[1].astype(jnp.int32)
    places = (jnp.arange(COL_DEV, dtype=jnp.int32)[:, None] * (P_SIZE - 1) + jnp.arange(P_SIZE - 1, dtype=jnp.int32)[None, :]) % others
    shifts = jnp.take(ordering, places.reshape(-1), axis=2).reshape((groups, LEV, COL_DEV, P_SIZE - 1)) + 1
    homes = jnp.arange(groups, dtype=jnp.int32)[:, None, None, None]
    target_group = (homes + shifts) % groups
    within = jax.random.randint(key_within, (groups, LEV, COL_DEV, P_SIZE - 1), 0, COL_DEV)
    remote = (target_group * COL_DEV + within).astype(jnp.int32)
    remote = jnp.moveaxis(remote, 2, 1).reshape((NCOL, LEV, P_SIZE - 1))
    own_column = jnp.broadcast_to(jnp.arange(NCOL, dtype=jnp.int32)[:, None, None], (NCOL, LEV, 1))
    return jnp.concatenate([own_column, remote], axis=2).astype(jnp.int32)


def with_ends(values, rng, least, high):
    place = [jax.random.randint(jax.random.fold_in(rng, axis), (), 0, length) for axis, length in enumerate(values.shape)]
    widest = values.shape.index(max(values.shape))
    neighbour = place[:widest] + [(place[widest] + 1) % values.shape[widest]] + place[widest + 1:]
    return values.at[tuple(place)].set(least).at[tuple(neighbour)].set(high)


def level_of(stream_key, extent, cuts, least, high):
    loudness = 1.0
    for axis_at, parts in cuts:
        steps = jax.random.uniform(jax.random.fold_in(jax.random.fold_in(stream_key, 6), axis_at), (parts,), jnp.float32, least / len(cuts), high / len(cuts))
        loudness = loudness * jnp.repeat(jnp.exp(steps), extent[axis_at] // parts).reshape((-1,) + (1,) * (len(extent) - 1 - axis_at))
    return loudness


def scatter_about(rng, extent, scale, most, pieces=(), kind=jnp.bfloat16):
    values = jax.random.normal(rng, extent, jnp.float32) * scale
    if len(pieces) > 0:
        values = level_of(rng, extent, pieces, -0.22, 0.18) * values
    return jnp.clip(values, min=-most, max=most).astype(kind)


def setup_inputs(seed: int = 0) -> dict:
    key_list = jax.random.split(jax.random.key(seed), 7)
    return {
        "ensemble": scatter_about(key_list[0], (K, NCOL, LEV, BS), 1.0, 6.0, ((0, 8), (1, 32))),
        "obs_values": scatter_about(key_list[1], (NCOL, LEV, OB), 1.5, 9.0, ((0, 32), (1, 8)), jnp.float32),
        "obs_var": jnp.clip(jnp.exp(math.log(4.0) - 2.7725887 * jax.random.uniform(key_list[2], (NCOL, LEV, OB), jnp.float32) ** level_of(key_list[2], (NCOL, LEV, OB), ((0, 32), (1, 8)), -0.2, 0.2)), 0.25, 4.0),
        "obs_cols": with_ends(jax.random.randint(key_list[3], (NCOL, LEV, OB), 0, BS), jax.random.fold_in(key_list[3], 1), 0, BS - 1).astype(jnp.int32),
        "obs_counts": draw_obs_counts(jax.random.fold_in(key_list[6], 71), 0),
        "pattern": draw_pattern(jax.random.fold_in(key_list[6], 71), 0),
    }


def taper_rows(pattern, own_columns, anchor, row_total, all_columns):
    batch_columns = anchor + jnp.arange(row_total, dtype=jnp.int32)
    chosen = lax.dynamic_slice_in_dim(pattern, anchor, row_total, 0)
    matches = lax.optimization_barrier(jnp.sum((chosen[None] == own_columns[:, None, None, None]).astype(jnp.float32), axis=3))
    spacing = jnp.abs(own_columns[:, None] - batch_columns[None, :])
    spacing = jnp.minimum(spacing, all_columns - spacing).astype(jnp.float32)
    radius = 2.0 * spacing / all_columns
    weight = (((-0.25 * radius + 0.5) * radius + 0.625) * radius - 5.0 / 3.0) * radius * radius + 1.0
    return (matches * weight[:, :, None]).astype(jnp.bfloat16)

def invert_all(system, order):
    flat = system.reshape((-1, order, order))
    identity = jnp.eye(order, dtype=jnp.float32)

    def invert_one(matrix):
        factor = jnp.linalg.cholesky(matrix)
        return jax.scipy.linalg.cho_solve((factor, True), identity)
    return jax.vmap(invert_one)(flat).reshape(system.shape)

def analyse_level(inputs):
    states, values, variances, columns, counts, taper = inputs
    identity = jnp.eye(K, dtype=jnp.float32)
    ens_mean = lax.optimization_barrier(jnp.sum(states, axis=0, dtype=jnp.float32)) / K
    anomalies = (states - ens_mean).astype(jnp.bfloat16)
    observed = jnp.take_along_axis(anomalies, columns[None], axis=2)
    mean_seen = jnp.take_along_axis(ens_mean, columns, axis=1)
    live_slots = (jnp.arange(OB, dtype=jnp.int32)[None, :] < counts[:, None]).astype(jnp.float32)
    obs_spread = jnp.sqrt(variances)
    weighted = (jnp.moveaxis(observed, 0, 1).astype(jnp.float32) * (live_slots / obs_spread)[:, None, :]).astype(jnp.bfloat16)
    residual_obs = (live_slots * (values - mean_seen) / obs_spread).astype(jnp.bfloat16)
    widened = weighted.astype(jnp.float32)
    products = jnp.einsum('bko,bmo->bkm', widened, widened).astype(jnp.bfloat16)
    projected = jnp.einsum('bko,bo->bk', widened, residual_obs.astype(jnp.float32)).astype(jnp.bfloat16)
    taper_wide = taper.astype(jnp.float32)
    system_sum = jnp.einsum('sb,bkm->skm', taper_wide, products.astype(jnp.float32)) + (K - 1) * identity
    right_sum = jnp.einsum('sb,bk->sk', taper_wide, projected.astype(jnp.float32))
    inverse = invert_all(system_sum, K)
    weights = jnp.einsum('skm,sm->sk', inverse, right_sum, precision=lax.Precision.HIGHEST)
    transform = (0.5 * identity + 0.5 * (K - 1) * inverse + weights[:, None, :]).astype(jnp.bfloat16)
    increment = jnp.einsum('skj,jsb->ksb', transform.astype(jnp.float32), anomalies.astype(jnp.float32))
    return (ens_mean + increment).astype(jnp.bfloat16)

def reference(ensemble, obs_values, obs_var, obs_cols, obs_counts, pattern):
    own_columns = jnp.arange(NCOL, dtype=jnp.int32)
    taper_all = taper_rows(pattern, own_columns, 0, NCOL, NCOL)
    stacked = (jnp.moveaxis(ensemble, 2, 0), jnp.moveaxis(obs_values, 1, 0), jnp.moveaxis(obs_var, 1, 0), jnp.moveaxis(obs_cols, 1, 0), jnp.moveaxis(obs_counts, 1, 0), jnp.moveaxis(taper_all, 2, 0))
    result = lax.map(analyse_level, stacked)
    return jnp.moveaxis(result, 0, 2)
```

```python
import functools

import jax
import jax.numpy as jnp
from jax import lax
from jax.experimental import pallas as pl
from jax.experimental.pallas import tpu as pltpu
from jax.sharding import PartitionSpec as P

F32 = jnp.float32
BF16 = jnp.bfloat16
MESH = pl.DeviceIdType.MESH

K = 160
BS = 128
NZ = 8
MZ = 20
ROWS = 320
WROWS = 336
TROWS = 480
NB = 32
VMEM_LIMIT = 48 * 1024 * 1024


def params(**more):
    return pltpu.CompilerParams(vmem_limit_bytes=VMEM_LIMIT, **more)


def swap_mem_kernel(x_ref, o_ref, send_sem, recv_sem, own_sem):
    n = NZ
    me = lax.axis_index("mem")
    barrier = pltpu.get_barrier_semaphore()
    for i in range(1, n):
        pl.semaphore_signal(
            barrier, inc=1, device_id={"mem": lax.rem(me + i, n)}, device_id_type=MESH
        )
    pl.semaphore_wait(barrier, n - 1)
    copies = []
    for i in (4, 3, 5, 2, 6, 1, 7):
        to = lax.rem(me + i, n)
        copy = pltpu.make_async_remote_copy(
            src_ref=x_ref.at[to],
            dst_ref=o_ref.at[me],
            send_sem=send_sem.at[i],
            recv_sem=recv_sem.at[i],
            device_id={"mem": to},
            device_id_type=MESH,
        )
        copy.start()
        copies.append(copy)
    own = pltpu.make_async_copy(x_ref.at[me], o_ref.at[me], own_sem)
    own.start()
    own.wait()
    for copy in copies:
        copy.wait()


def swap_mem(x, ident):
    return pl.pallas_call(
        swap_mem_kernel,
        out_shape=jax.ShapeDtypeStruct(x.shape, x.dtype),
        in_specs=[pl.BlockSpec(memory_space=pl.ANY)],
        out_specs=pl.BlockSpec(memory_space=pl.ANY),
        scratch_shapes=[
            pltpu.SemaphoreType.DMA((NZ,)),
            pltpu.SemaphoreType.DMA((NZ,)),
            pltpu.SemaphoreType.DMA,
        ],
        compiler_params=params(collective_id=ident, has_side_effects=True),
        name="swap_mem",
    )(x)


def chip_of(index):
    return index // 8, lax.rem(index // 2, 4), lax.rem(index, 2)


def level_at(x, y):
    return lax.rem(x, 2) * 4 + y


def spread_kernel(w_ref, o_ref, send_sem, recv_sem, send_pair, recv_pair, own_sem):
    me = lax.axis_index("dom")
    x, y, c = chip_of(me)
    pair = x * 8 + y * 2 + (1 - c)
    offsets = sorted(
        ((dx, dy) for dx in range(4) for dy in range(4) if (dx, dy) != (0, 0)),
        key=lambda o: (min(o[0], 4 - o[0]) + min(o[1], 4 - o[1]), o),
    )

    def chip_at(dx, dy):
        return lax.rem(x + dx, 4), lax.rem(y + dy, 4)

    barrier = pltpu.get_barrier_semaphore()
    for dx, dy in offsets:
        tx, ty = chip_at(dx, dy)
        pl.semaphore_signal(
            barrier, inc=1, device_id={"dom": tx * 8 + ty * 2 + c}, device_id_type=MESH
        )
    pl.semaphore_signal(barrier, inc=1, device_id={"dom": pair}, device_id_type=MESH)
    pl.semaphore_wait(barrier, 16)

    own_level = level_at(x, y)
    first = []
    for dx, dy in reversed(offsets):
        tx, ty = chip_at(dx, dy)
        copy = pltpu.make_async_remote_copy(
            src_ref=w_ref.at[level_at(tx, ty)],
            dst_ref=o_ref.at[me],
            send_sem=send_sem.at[dx * 4 + dy],
            recv_sem=recv_sem.at[dx * 4 + dy],
            device_id={"dom": tx * 8 + ty * 2 + c},
            device_id_type=MESH,
        )
        copy.start()
        first.append((dx, dy, copy))
    second = pltpu.make_async_remote_copy(
        src_ref=w_ref.at[own_level],
        dst_ref=o_ref.at[me],
        send_sem=send_pair.at[0],
        recv_sem=recv_pair.at[0],
        device_id={"dom": pair},
        device_id_type=MESH,
    )
    second.start()
    later = [second]
    own = pltpu.make_async_copy(w_ref.at[own_level], o_ref.at[me], own_sem)
    own.start()
    for dx, dy, copy in reversed(first):
        copy.wait_recv()
        sx, sy = chip_at(4 - dx, 4 - dy)
        slot = sx * 8 + sy * 2 + c
        onward = pltpu.make_async_remote_copy(
            src_ref=o_ref.at[slot],
            dst_ref=o_ref.at[slot],
            send_sem=send_pair.at[dx * 4 + dy],
            recv_sem=recv_pair.at[dx * 4 + dy],
            device_id={"dom": pair},
            device_id_type=MESH,
        )
        onward.start()
        later.append(onward)
    own.wait()
    for _, _, copy in first:
        copy.wait_send()
    for onward in later:
        onward.wait()


def spread(weighted):
    return pl.pallas_call(
        spread_kernel,
        out_shape=jax.ShapeDtypeStruct((32, WROWS, BS), BF16),
        in_specs=[pl.BlockSpec(memory_space=pl.ANY)],
        out_specs=pl.BlockSpec(memory_space=pl.ANY),
        scratch_shapes=[pltpu.SemaphoreType.DMA((16,))] * 4 + [pltpu.SemaphoreType.DMA],
        compiler_params=params(collective_id=1, has_side_effects=True),
        name="spread",
    )(weighted)


def swap_plane_kernel(t_ref, o_ref, send_sem, recv_sem, own_sem):
    me = lax.axis_index("dom")
    x, y, c = chip_of(me)
    base = (x // 2) * 2
    mine = level_at(x, y)

    def member(g):
        return (base + g // 4) * 8 + lax.rem(g, 4) * 2 + c

    barrier = pltpu.get_barrier_semaphore()
    for i in range(1, 8):
        pl.semaphore_signal(
            barrier,
            inc=1,
            device_id={"dom": member(lax.rem(mine + i, 8))},
            device_id_type=MESH,
        )
    pl.semaphore_wait(barrier, 7)
    copies = []
    for i in range(1, 8):
        to = lax.rem(mine + i, 8)
        copy = pltpu.make_async_remote_copy(
            src_ref=t_ref.at[to],
            dst_ref=o_ref.at[mine],
            send_sem=send_sem.at[i],
            recv_sem=recv_sem.at[i],
            device_id={"dom": member(to)},
            device_id_type=MESH,
        )
        copy.start()
        copies.append(copy)
    own = pltpu.make_async_copy(t_ref.at[mine], o_ref.at[mine], own_sem)
    own.start()
    own.wait()
    for copy in copies:
        copy.wait()


def swap_plane(t):
    return pl.pallas_call(
        swap_plane_kernel,
        out_shape=jax.ShapeDtypeStruct(t.shape, t.dtype),
        in_specs=[pl.BlockSpec(memory_space=pl.ANY)],
        out_specs=pl.BlockSpec(memory_space=pl.ANY),
        scratch_shapes=[
            pltpu.SemaphoreType.DMA((8,)),
            pltpu.SemaphoreType.DMA((8,)),
            pltpu.SemaphoreType.DMA,
        ],
        compiler_params=params(collective_id=2, has_side_effects=True),
        name="swap_plane",
    )(t)


def dot(a, b):
    return jnp.dot(a, b, preferred_element_type=F32)


def observe_kernel(e_ref, val_ref, var_ref, col_ref, cnt_ref, w_ref, a_ref, m_ref, wide):
    for z in range(NZ):
        wide[pl.ds(z * ROWS, ROWS), :] = e_ref[z].astype(F32)
    sub = lax.broadcasted_iota(jnp.int32, (BS, BS), 0)
    lane = lax.broadcasted_iota(jnp.int32, (1, BS), 1)
    row16 = lax.broadcasted_iota(jnp.int32, (16, BS), 0)
    for l in range(8):
        tail = jnp.zeros((16, BS), F32)
        for c in range(2):
            cl = c * 8 + l
            states = wide[pl.ds(cl, K, stride=16), :]
            mean = jnp.sum(states, axis=0, keepdims=True) / K
            anom = (states - mean).astype(BF16)
            a_ref[cl] = anom
            m_ref[pl.ds(cl, 1), :] = mean
            high = mean.astype(BF16)
            rest = mean - high.astype(F32)
            mid = rest.astype(BF16)
            low = (rest - mid.astype(F32)).astype(BF16)
            parts = jnp.where(
                row16 == 0,
                high.astype(F32),
                jnp.where(row16 == 1, mid.astype(F32), jnp.where(row16 == 2, low.astype(F32), 0.0)),
            ).astype(BF16)
            picked = (sub == col_ref[c, pl.ds(l, 1), :]).astype(F32).astype(BF16)
            seen = dot(jnp.concatenate([anom, parts], axis=0), picked)
            live = (lane < cnt_ref[c, l]).astype(F32)
            spread_ = jnp.sqrt(var_ref[c, pl.ds(l, 1), :])
            w_ref[l, pl.ds(c * K, K), :] = (seen[:K] * (live / spread_)).astype(BF16)
            mean_seen = seen[K : K + 1] + seen[K + 1 : K + 2] + seen[K + 2 : K + 3]
            resid = live * (val_ref[c, pl.ds(l, 1), :] - mean_seen) / spread_
            tail = jnp.where(row16 == c, resid, tail)
        w_ref[l, pl.ds(2 * K, 16), :] = tail.astype(BF16)


def observe(e, values, variances, columns, counts):
    vmem = pl.BlockSpec(memory_space=pltpu.VMEM)
    return pl.pallas_call(
        observe_kernel,
        out_shape=(
            jax.ShapeDtypeStruct((8, WROWS, BS), BF16),
            jax.ShapeDtypeStruct((16, K, BS), BF16),
            jax.ShapeDtypeStruct((16, BS), F32),
        ),
        in_specs=[vmem] * 4 + [pl.BlockSpec(memory_space=pltpu.SMEM)],
        out_specs=(vmem, vmem, vmem),
        scratch_shapes=[pltpu.VMEM((NZ * ROWS, BS), F32)],
        compiler_params=params(),
        name="observe",
    )(e, values, variances, columns, counts)


def apply_kernel(t_ref, a_ref, m_ref, o_ref, wide):
    none = jnp.zeros((NB, BS), BF16)
    for l in range(8):
        shared = t_ref[l, pl.ds(2 * K, K), :]
        for c in range(2):
            cl = c * 8 + l
            anom = a_ref[cl]
            rest = [none] * 4
            rest[c] = anom[BS:]
            left = jnp.concatenate([t_ref[l, pl.ds(c * K, K), :], shared], axis=1)
            right = jnp.concatenate([anom[:BS]] + rest, axis=0)
            wide[pl.ds(cl, K, stride=16), :] = m_ref[pl.ds(cl, 1), :] + dot(left, right)
    for z in range(NZ):
        o_ref[z] = wide[pl.ds(z * ROWS, ROWS), :].astype(BF16)


def apply_transform(t, anomalies, means):
    vmem = pl.BlockSpec(memory_space=pltpu.VMEM)
    return pl.pallas_call(
        apply_kernel,
        out_shape=jax.ShapeDtypeStruct((NZ, ROWS, BS), BF16),
        in_specs=[vmem] * 3,
        out_specs=vmem,
        scratch_shapes=[pltpu.VMEM((NZ * ROWS, BS), F32)],
        compiler_params=params(),
        name="apply",
    )(t, anomalies, means)


def left_parts(v, seg):
    lane = lax.broadcasted_iota(jnp.int32, v.shape, 1) // NB
    high = v.astype(BF16).astype(F32)
    low = v - high
    out = jnp.where(lane == seg, high, 0.0)
    out = jnp.where(lane == (seg + 1) % 4, pltpu.roll(high, NB, 1), out)
    out = jnp.where(lane == (seg + 2) % 4, pltpu.roll(low, 2 * NB, 1), out)
    return out.astype(BF16)


def right_parts(v, seg):
    high = v.astype(BF16)
    low = (v - high.astype(F32)).astype(BF16)
    order = [None] * 4
    order[seg] = high
    order[(seg + 1) % 4] = low
    order[(seg + 2) % 4] = high
    order[(seg + 3) % 4] = jnp.zeros_like(high)
    return jnp.concatenate(order, axis=0)


def invert_blocks(packs):
    shape = packs[0].shape
    row = lax.broadcasted_iota(jnp.int32, shape, 0)
    lane = lax.broadcasted_iota(jnp.int32, shape, 1)
    seg_start = (lane // NB) * NB
    within = lane % NB
    group = 8
    for start in range(0, NB, group):
        columns = [
            [
                jnp.take_along_axis(p, seg_start + (start + q), axis=1, mode="promise_in_bounds")
                for q in range(group)
            ]
            for p in packs
        ]
        for q in range(group):
            j = start + q
            at_row = row == j
            at_lane = within == j
            fresh = []
            for g, p in enumerate(packs):
                cols = columns[g]
                column = cols[q]
                inv = 1.0 / column[j : j + 1, :]
                others = jnp.where(at_row, 0.0, column)
                p = jnp.where(at_lane, jnp.where(at_row, 1.0, 0.0), p)
                scaled = p[j : j + 1, :] * inv
                fresh.append(jnp.where(at_row, scaled, p - others * scaled))
                for r in range(q + 1, group):
                    line = cols[r][j : j + 1, :] * inv
                    cols[r] = jnp.where(at_row, line, cols[r] - others * line)
            packs = fresh
    return packs


def solve_kernel(idx_ref, wt_ref, cnt_ref, w_ref, o_ref, prod, mat, inv_ref):
    row16 = lax.broadcasted_iota(jnp.int32, (16, BS), 0)

    def product(home, _):
        tail = w_ref[home, pl.ds(2 * K, 16), :]
        for c in range(2):
            w = w_ref[home, pl.ds(c * K, K), :]
            resid = jnp.where(row16 == c, tail.astype(F32), 0.0).astype(BF16)
            left = jnp.concatenate([w, resid], axis=0)
            full = lax.dot_general(
                left, w, (((1,), (1,)), ((), ())), preferred_element_type=F32
            ).astype(BF16)
            prod[2 * home + c, :, pl.ds(0, BS)] = full[:, :BS]
            prod[2 * home + c, :, pl.ds(BS, NB)] = full[:, BS:]
        return 0

    lax.fori_loop(0, 32, product, 0)

    sub = lax.broadcasted_iota(jnp.int32, (176, BS), 0)
    lane = lax.broadcasted_iota(jnp.int32, (176, BS), 1)
    eye_a = jnp.where(sub == lane, K - 1.0, 0.0)
    eye_b = jnp.where((sub == lane + BS) & (sub < K), K - 1.0, 0.0)

    def gather(s, _):
        def add(n, carry):
            b = idx_ref[s, n]
            t = wt_ref[s, n]
            a, rest = carry
            a = a + t * prod[b, :, pl.ds(0, BS)].astype(F32)
            rest = rest + t * prod[b, :, pl.ds(BS, BS)].astype(F32)
            return a, rest

        a, rest = lax.fori_loop(0, cnt_ref[s], add, (eye_a, eye_b))
        live = lane[:K] < NB
        mat[s, pl.ds(0, K), pl.ds(0, BS)] = a[:K]
        mat[s, pl.ds(0, K), pl.ds(BS, BS)] = jnp.where(live, rest[:K], 0.0)
        ra = jnp.sum(a[K : K + 8], axis=0, keepdims=True)
        rb = jnp.sum(jnp.where(live[:8], rest[K : K + 8], 0.0), axis=0, keepdims=True)
        mat[s, pl.ds(K, 8), pl.ds(0, BS)] = jnp.broadcast_to(ra, (8, BS))
        mat[s, pl.ds(K, 8), pl.ds(BS, BS)] = jnp.broadcast_to(rb, (8, BS))
        return 0

    lax.fori_loop(0, 16, gather, 0)

    lane_b = lax.broadcasted_iota(jnp.int32, (NB, BS), 1)
    sub_b = lax.broadcasted_iota(jnp.int32, (NB, BS), 0)
    lane_f = lax.broadcasted_iota(jnp.int32, (K + 8, BS), 1)
    for k in range(K // NB):
        tile, seg = (k * NB) // BS, k % 4
        packs = []
        for g in range(4):
            pack = jnp.zeros((NB, BS), F32)
            for q in range(4):
                block = mat[4 * g + q, pl.ds(k * NB, NB), pl.ds(tile * BS, BS)]
                if q != seg:
                    block = pltpu.roll(block, ((q - seg) * NB) % BS, 1)
                pack = jnp.where(lane_b // NB == q, block, pack)
            packs.append(pack)
        packs = invert_blocks(packs)
        for g in range(4):
            for q in range(4):
                inv_ref[4 * g + q] = left_parts(packs[g], q)

        at_seg = lane_b // NB == seg
        eye_seg = jnp.where(at_seg & (sub_b == lane_b - seg * NB), 1.0, 0.0)

        def eliminate(s4, _):
            for q in range(4):
                s = s4 * 4 + q
                panel = [mat[s, pl.ds(k * NB, NB), pl.ds(t * BS, BS)] for t in range(2)]
                panel[tile] = jnp.where(at_seg, eye_seg, panel[tile])
                scaled = dot(inv_ref[s], right_parts(jnp.concatenate(panel, axis=1), q))
                left = left_parts(mat[s, :, pl.ds(tile * BS, BS)], seg)
                taken = dot(left, right_parts(scaled, seg))
                for t in range(2):
                    old = mat[s, :, pl.ds(t * BS, BS)]
                    if t == tile:
                        old = jnp.where(lane_f // NB == seg, 0.0, old)
                    mat[s, :, pl.ds(t * BS, BS)] = old - taken[:, t * BS : (t + 1) * BS]
                mat[s, pl.ds(k * NB, NB), :] = scaled
            return 0

        lax.fori_loop(0, 4, eliminate, 0)

    half = (K - 1) / 2.0
    diag_a = jnp.where(sub[:K] == lane[:K], 0.5, 0.0)
    diag_b = jnp.where(sub[:K] == lane[:K] + BS, 0.5, 0.0)

    def emit(h, _):
        joint = jnp.zeros((K, BS), F32)
        for c in range(2):
            s = 2 * h + c
            wa = mat[s, pl.ds(K, 1), pl.ds(0, BS)]
            wb = mat[s, pl.ds(K, 1), pl.ds(BS, BS)]
            ta = diag_a + half * mat[s, pl.ds(0, K), pl.ds(0, BS)] - wa
            tb = diag_b + half * mat[s, pl.ds(0, K), pl.ds(BS, BS)] - wb
            o_ref[h, pl.ds(c * K, K), :] = ta.astype(BF16)
            if c:
                tb = pltpu.roll(tb, NB, 1)
            joint = jnp.where(lane[:K] // NB == c, tb, joint)
        o_ref[h, pl.ds(2 * K, K), :] = joint.astype(BF16)
        return 0

    lax.fori_loop(0, 8, emit, 0)


def solve(indices, tapers, totals, weighted):
    vmem = pl.BlockSpec(memory_space=pltpu.VMEM)
    smem = pl.BlockSpec(memory_space=pltpu.SMEM)
    return pl.pallas_call(
        solve_kernel,
        out_shape=jax.ShapeDtypeStruct((8, TROWS, BS), BF16),
        in_specs=[smem, smem, smem, vmem],
        out_specs=vmem,
        scratch_shapes=[
            pltpu.VMEM((64, 176, 2 * BS), BF16),
            pltpu.VMEM((16, K + 8, 2 * BS), F32),
            pltpu.VMEM((16, NB, BS), BF16),
        ],
        compiler_params=params(),
        name="solve",
    )(indices, tapers, totals, weighted)


def pair_lists(pattern):
    x, y, c = chip_of(lax.axis_index("dom"))
    own = lax.dynamic_index_in_dim(pattern, level_at(x, y), 1, keepdims=False)
    home = jnp.arange(16, dtype=jnp.int32) // 2
    index = ((x // 2) * 2 + home // 4) * 8 + (home % 4) * 2 + c
    columns = index * 2 + jnp.arange(16, dtype=jnp.int32) % 2
    batches = jnp.arange(64, dtype=jnp.int32)
    matches = jnp.sum((own[None] == columns[:, None, None]).astype(F32), axis=2)
    spacing = jnp.abs(columns[:, None] - batches[None, :])
    spacing = jnp.minimum(spacing, 64 - spacing).astype(F32)
    radius = 2.0 * spacing / 64
    weight = (
        ((-0.25 * radius + 0.5) * radius + 0.625) * radius - 5.0 / 3.0
    ) * radius * radius + 1.0
    taper = (matches * weight).astype(BF16).astype(F32)
    upto = (batches[:, None] <= batches[None, :]).astype(F32)
    place = jnp.sum(matches[:, :, None] * upto[None], axis=1) - 1.0
    chosen = (place[:, None, :] == batches[None, :, None].astype(F32)) * matches[:, None, :]
    indices = jnp.sum(chosen * batches.astype(F32), axis=2).astype(jnp.int32)
    tapers = jnp.sum(chosen * taper[:, None, :], axis=2)
    totals = jnp.sum(matches, axis=1).astype(jnp.int32)
    return indices, tapers, totals


def per_device(ensemble, obs_values, obs_var, obs_cols, obs_counts, pattern):
    indices, tapers, totals = pair_lists(pattern)
    out = jnp.transpose(ensemble.reshape(MZ, 2, NZ, 8, BS), (2, 0, 1, 3, 4))
    states = swap_mem(out.reshape(NZ, ROWS, BS), 0)
    weighted, anomalies, means = observe(states, obs_values, obs_var, obs_cols, obs_counts)
    transforms = swap_plane(solve(indices, tapers, totals, spread(weighted)))
    analysed = swap_mem(apply_transform(transforms, anomalies, means), 3)
    back = jnp.transpose(analysed.reshape(NZ, MZ, 2, 8, BS), (1, 2, 0, 3, 4))
    return back.reshape(MZ, 2, 64, BS)


def solution(mesh):
    placed = (
        P("mem", "dom", None, None),
        P("dom", "mem", None),
        P("dom", "mem", None),
        P("dom", "mem", None),
        P("dom", "mem"),
        P(None, "mem", None),
    )
    return jax.shard_map(
        per_device,
        mesh=mesh,
        in_specs=placed,
        out_specs=P("mem", "dom", None, None),
        check_vma=False,
    )
```

```python
import jax
import jax.numpy as jnp
from jax import lax
from jax.experimental import pallas as pl
from jax.experimental.pallas import tpu as pltpu
from jax.sharding import PartitionSpec as P

F32 = jnp.float32
BF16 = jnp.bfloat16
MESH = pl.DeviceIdType.MESH

K = 160
BS = 128
NZ = 8
MZ = 20
ROWS = 160
WROWS = 176
TROWS = 208
NB = 32
UNROLL = 4
VMEM_LIMIT = 48 * 1024 * 1024


def params(**more):
    return pltpu.CompilerParams(vmem_limit_bytes=VMEM_LIMIT, **more)


def dot(a, b):
    return jnp.dot(a, b, preferred_element_type=F32)


def position():
    me = lax.axis_index("dom")
    return me // 8, lax.rem(me // 2, 4), lax.rem(me, 2)


def index_of(x, y, core):
    return lax.rem(x + 8, 4) * 8 + lax.rem(y + 8, 4) * 2 + core


def toward(x, y):
    return 2 * lax.rem(x + y + 8, 2) - 1


def level_at(x, y):
    x, y = lax.rem(x + 8, 4), lax.rem(y + 8, 4)
    return y * 2 + lax.rem(x + 3 * lax.rem(y, 2), 4) // 2


NEAR = [(k, dy) for dy in (0, 1, 3, 2) for k in (0, 1)]


def signal_dom(sem, index):
    pl.semaphore_signal(sem, inc=1, device_id={"dom": index}, device_id_type=MESH)


def push(src, dst, send_sem, recv_sem, **to):
    copy = pltpu.make_async_remote_copy(
        src_ref=src,
        dst_ref=dst,
        send_sem=send_sem,
        recv_sem=recv_sem,
        device_id=to,
        device_id_type=MESH,
    )
    copy.start()
    return copy


def stay(src, dst, sem):
    copy = pltpu.make_async_copy(src, dst, sem)
    copy.start()
    return copy


def observe_column(c, e_ref, val_ref, var_ref, col_ref, cnt_ref, w_ref, a_ref, m_ref, wide):
    for z in range(NZ):
        wide[pl.ds(z * ROWS, ROWS), :] = e_ref[c, z].astype(F32)
    sub = lax.broadcasted_iota(jnp.int32, (BS, BS), 0)
    lane = lax.broadcasted_iota(jnp.int32, (1, BS), 1)
    row16 = lax.broadcasted_iota(jnp.int32, (16, BS), 0)
    for l in range(8):
        cl = c * 8 + l
        states = wide[pl.ds(l, K, stride=8), :]
        mean = jnp.sum(states, axis=0, keepdims=True) / K
        anom = (states - mean).astype(BF16)
        a_ref[cl] = anom
        m_ref[pl.ds(cl, 1), :] = mean
        high = mean.astype(BF16)
        rest = mean - high.astype(F32)
        mid = rest.astype(BF16)
        low = (rest - mid.astype(F32)).astype(BF16)
        parts = jnp.where(
            row16 == 0,
            high.astype(F32),
            jnp.where(row16 == 1, mid.astype(F32), jnp.where(row16 == 2, low.astype(F32), 0.0)),
        ).astype(BF16)
        picked = (sub == col_ref[c, pl.ds(l, 1), :]).astype(F32).astype(BF16)
        seen = dot(jnp.concatenate([anom, parts], axis=0), picked)
        live = (lane < cnt_ref[c, l]).astype(F32)
        spread = jnp.sqrt(var_ref[c, pl.ds(l, 1), :])
        w_ref[c, l, pl.ds(0, K), :] = (seen[:K] * (live / spread)).astype(BF16)
        mean_seen = seen[K : K + 1] + seen[K + 1 : K + 2] + seen[K + 2 : K + 3]
        resid = live * (val_ref[c, pl.ds(l, 1), :] - mean_seen) / spread
        w_ref[c, l, pl.ds(K, 16), :] = jnp.where(row16 == 0, resid, 0.0).astype(BF16)


class Swap:
    def __init__(self, source, target, relay, send_sem, recv_sem, own_sem):
        self.z = lax.axis_index("mem")
        self.source, self.target, self.relay = source, target, relay
        self.send_sem, self.recv_sem, self.own_sem = send_sem, recv_sem, own_sem

    def push(self, src, dst, n, to):
        return push(src, dst, self.send_sem.at[n], self.recv_sem.at[n], mem=to)

    def begin(self):
        z = self.z
        opposite = self.source.at[lax.rem(z + 4, NZ)]
        low, high = pl.ds(0, ROWS // 2), pl.ds(ROWS // 2, ROWS // 2)
        self.leg = self.push(opposite.at[high], self.relay, 0, lax.rem(z + 6, NZ))
        self.copies = [
            self.push(opposite.at[low], self.target.at[z, low], 4, lax.rem(z + 4, NZ))
        ]
        for i in (5, 3, 6, 2, 7, 1):
            to = lax.rem(z + i, NZ)
            self.copies.append(self.push(self.source.at[to], self.target.at[z], i, to))
        self.own = stay(self.source.at[z], self.target.at[z], self.own_sem)

    def forward(self):
        z = self.z
        self.leg.wait_recv()
        high = pl.ds(ROWS // 2, ROWS // 2)
        self.copies.append(
            self.push(self.relay, self.target.at[lax.rem(z + 2, NZ), high], 8, lax.rem(z + 6, NZ))
        )

    def arrive(self):
        for copy in self.copies:
            copy.wait_recv()
        self.own.wait()

    def finish(self):
        self.leg.wait_send()
        for copy in self.copies:
            copy.wait_send()


def greet_mem(barrier):
    z = lax.axis_index("mem")
    for i in range(1, NZ):
        pl.semaphore_signal(
            barrier, inc=1, device_id={"mem": lax.rem(z + i, NZ)}, device_id_type=MESH
        )


def forward_kernel(
    ens_ref, val_ref, var_ref, col_ref, cnt_ref,
    prod_ref, a_ref, m_ref,
    ens, x_buf, e_buf, relay, wide, w_buf, wall, prod,
    z_send, z_recv, n_send, n_recv, f_send, f_recv, p_send, p_recv, own_sem, out_sem,
):
    me = lax.axis_index("dom")
    x, y, core = position()
    e = toward(x, y)
    partner = index_of(x - e, y, core)
    sibling = index_of(x, y, 1 - core)
    mine = level_at(x, y)

    load = stay(ens_ref, ens, out_sem.at[0])
    barrier = pltpu.get_barrier_semaphore()
    greet_mem(barrier)
    for k, dy in NEAR[1:]:
        signal_dom(barrier, index_of(x + k * e, y - dy, core))
    signal_dom(barrier, partner)
    signal_dom(barrier, sibling)

    def regroup(c):
        for j in range(NZ // 2):
            rows = ens[:, c, pl.ds(16 * j, 16), :].astype(F32)
            for half in range(2):
                part = rows[:, 8 * half : 8 * half + 8].reshape(ROWS, BS)
                x_buf[c, 2 * j + half] = part.astype(BF16)

    direct, relayed, paired, owns = [{}, {}], [{}, {}], [{}, {}], []

    def to_sibling(c, n, src, slot):
        paired[c][n] = push(
            src, wall.at[c, slot], p_send.at[c, n], p_recv.at[c, n], dom=sibling
        )

    def to_partner(c, n, src, slot):
        relayed[c][n] = push(
            src, wall.at[c, slot], f_send.at[c, n], f_recv.at[c, n], dom=partner
        )

    def send_near(c):
        for k, dy in reversed(NEAR[1:]):
            tx, ty = x + k * toward(x, y + dy), y + dy
            direct[c][k, dy] = push(
                w_buf.at[c, level_at(tx, ty)],
                wall.at[c, me],
                n_send.at[c, k * 4 + dy],
                n_recv.at[c, k * 4 + dy],
                dom=index_of(tx, ty, core),
            )
        source = w_buf.at[c, mine]
        to_partner(c, 0, source, me)
        to_sibling(c, 0, source, me)
        owns.append(stay(source, wall.at[c, me], own_sem.at[2 + c]))

    def from_near(c, k, dy):
        direct[c][k, dy].wait_recv()
        slot = index_of(x + k * e, y - dy, core)
        to_partner(c, k * 4 + dy, wall.at[c, slot], slot)
        to_sibling(c, k * 4 + dy, wall.at[c, slot], slot)

    def from_partner(c, k, dy):
        relayed[c][k * 4 + dy].wait_recv()
        slot = index_of(x - e - k * e, y - dy, core)
        to_sibling(c, 8 + k * 4 + dy, wall.at[c, slot], slot)

    def multiply(c, which, n):
        slot = 2 * n + (core if which == 0 else 1 - core)
        full = lax.dot_general(
            wall[c, slot], wall[c, slot, pl.ds(0, K), :],
            (((1,), (1,)), ((), ())),
            preferred_element_type=F32,
        )
        full = jnp.concatenate([full, jnp.zeros((WROWS, 2 * BS - K), F32)], axis=1)
        prod[c, which, n] = full.astype(BF16)

    def multiply_all(c, which):
        def body(n, _):
            multiply(c, which, n)
            return 0

        lax.fori_loop(0, 16, body, 0, unroll=UNROLL)

    outs = []

    def write(c, which):
        n = c * 2 + which
        outs.append(stay(prod.at[c, which], prod_ref.at[c, which], out_sem.at[n]))

    swaps = [
        Swap(
            x_buf.at[c], e_buf.at[c], relay.at[c], z_send.at[c], z_recv.at[c], own_sem.at[c]
        )
        for c in range(2)
    ]

    def observe(c):
        observe_column(
            c, e_buf, val_ref, var_ref, col_ref, cnt_ref, w_buf, a_ref, m_ref, wide
        )
        send_near(c)

    load.wait()
    regroup(0)
    pl.semaphore_wait(barrier, NZ - 1 + 9)
    swaps[0].begin()
    regroup(1)
    swaps[0].forward()
    swaps[0].finish()
    swaps[1].begin()
    swaps[0].arrive()
    observe(0)
    swaps[1].forward()
    for k, dy in NEAR[1:]:
        from_near(0, k, dy)
    swaps[1].arrive()
    observe(1)
    for k, dy in NEAR:
        from_partner(0, k, dy)
    owns[0].wait()
    for n, (k, dy) in enumerate(NEAR):
        if n:
            from_near(1, k, dy)
        multiply(0, 0, 2 * n)
        multiply(0, 0, 2 * n + 1)
    write(0, 0)
    for copy in paired[0].values():
        copy.wait_recv()
    for n, (k, dy) in enumerate(NEAR):
        from_partner(1, k, dy)
        multiply(0, 1, 2 * n)
        multiply(0, 1, 2 * n + 1)
    write(0, 1)
    owns[1].wait()
    multiply_all(1, 0)
    write(1, 0)
    for copy in paired[1].values():
        copy.wait_recv()
    multiply_all(1, 1)
    write(1, 1)
    swaps[1].finish()
    for c in range(2):
        for group in (direct[c], relayed[c], paired[c]):
            for copy in group.values():
                copy.wait_send()
    for copy in outs:
        copy.wait()


def forward(x, values, variances, columns, counts):
    vmem = pl.BlockSpec(memory_space=pltpu.VMEM)
    anyw = pl.BlockSpec(memory_space=pl.ANY)
    dma = pltpu.SemaphoreType.DMA
    return pl.pallas_call(
        forward_kernel,
        out_shape=(
            jax.ShapeDtypeStruct((2, 2, 16, WROWS, 2 * BS), BF16),
            jax.ShapeDtypeStruct((16, K, BS), BF16),
            jax.ShapeDtypeStruct((16, BS), F32),
        ),
        in_specs=[anyw] + [vmem] * 3 + [pl.BlockSpec(memory_space=pltpu.SMEM)],
        out_specs=(anyw, vmem, vmem),
        scratch_shapes=[
            pltpu.VMEM((MZ, 2, 64, BS), BF16),
            pltpu.VMEM((2, NZ, ROWS, BS), BF16),
            pltpu.VMEM((2, NZ, ROWS, BS), BF16),
            pltpu.VMEM((2, ROWS // 2, BS), BF16),
            pltpu.VMEM((NZ * ROWS, BS), F32),
            pltpu.VMEM((2, 8, WROWS, BS), BF16),
            pltpu.VMEM((2, 32, WROWS, BS), BF16),
            pltpu.VMEM((2, 2, 16, WROWS, 2 * BS), BF16),
            dma((2, 9)), dma((2, 9)), dma((2, 8)), dma((2, 8)), dma((2, 8)), dma((2, 8)),
            dma((2, 16)), dma((2, 16)), dma((4,)), dma((4,)),
        ],
        compiler_params=params(collective_id=0, has_side_effects=True),
        name="forward",
    )(x, values, variances, columns, counts)


def back_kernel(
    t_ref, a_ref, m_ref, o_ref,
    t_buf, wide, out_buf, relay,
    n_send, n_recv, z_send, z_recv, own_sem,
):
    x, y, core = position()
    e = toward(x, y)
    mine = level_at(x, y)

    barrier = pltpu.get_barrier_semaphore()
    greet_mem(barrier)
    for k, dy in NEAR[1:]:
        signal_dom(barrier, index_of(x + k * toward(x, y - dy), y - dy, core))
    pl.semaphore_wait(barrier, NZ - 1 + 7)

    returns, owns = [], []

    def give(c):
        returns.append([])
        for k, dy in reversed(NEAR[1:]):
            n = k * 4 + dy
            returns[c].append(
                push(
                    t_ref.at[c, k * 4 + lax.rem(y + dy, 4)],
                    t_buf.at[c, mine],
                    n_send.at[c, n],
                    n_recv.at[c, n],
                    dom=index_of(x + k * e, y + dy, core),
                )
            )
        owns.append(stay(t_ref.at[c, y], t_buf.at[c, mine], own_sem.at[c]))

    none = jnp.zeros((BS - NB, BS), BF16)

    def apply(c):
        for l in range(8):
            anom = a_ref[c * 8 + l]
            folded = t_buf[c, l, pl.ds(K, 48), :].astype(F32)[:40]
            opened = [folded] + [pltpu.roll(folded, BS - NB * g, 1) for g in range(1, 4)]
            rest = jnp.concatenate(opened, axis=0).astype(BF16)
            left = jnp.concatenate([t_buf[c, l, pl.ds(0, K), :], rest], axis=1)
            right = jnp.concatenate([anom, none], axis=0)
            wide[pl.ds(l, K, stride=8), :] = m_ref[pl.ds(c * 8 + l, 1), :] + dot(left, right)
        for g in range(NZ):
            out_buf[c, g] = wide[pl.ds(g * ROWS, ROWS), :].astype(BF16)

    swaps = [
        Swap(
            out_buf.at[c], o_ref.at[c], relay.at[c], z_send.at[c], z_recv.at[c], own_sem.at[2 + c]
        )
        for c in range(2)
    ]
    give(0)
    for copy in returns[0]:
        copy.wait_send()
    give(1)
    for c in range(2):
        for copy in returns[c]:
            copy.wait_recv()
        owns[c].wait()
        apply(c)
        swaps[c].begin()
        swaps[c].forward()
    for copy in returns[1]:
        copy.wait_send()
    for swap in swaps:
        swap.arrive()
        swap.finish()


def back(t, anomalies, means):
    vmem = pl.BlockSpec(memory_space=pltpu.VMEM)
    anyw = pl.BlockSpec(memory_space=pl.ANY)
    dma = pltpu.SemaphoreType.DMA
    return pl.pallas_call(
        back_kernel,
        out_shape=jax.ShapeDtypeStruct((2, NZ, ROWS, BS), BF16),
        in_specs=[anyw, vmem, vmem],
        out_specs=anyw,
        scratch_shapes=[
            pltpu.VMEM((2, 8, TROWS, BS), BF16),
            pltpu.VMEM((NZ * ROWS, BS), F32),
            pltpu.VMEM((2, NZ, ROWS, BS), BF16),
            pltpu.VMEM((2, ROWS // 2, BS), BF16),
            dma((2, 8)), dma((2, 8)), dma((2, 9)), dma((2, 9)), dma((4,)),
        ],
        compiler_params=params(collective_id=1, has_side_effects=True),
        name="back",
    )(t, anomalies, means)


def left_parts(v, seg):
    lane = lax.broadcasted_iota(jnp.int32, v.shape, 1) // NB
    high = v.astype(BF16).astype(F32)
    low = v - high
    out = jnp.where(lane == seg, high, 0.0)
    out = jnp.where(lane == (seg + 1) % 4, pltpu.roll(high, NB, 1), out)
    out = jnp.where(lane == (seg + 2) % 4, pltpu.roll(low, 2 * NB, 1), out)
    return out.astype(BF16)


def right_parts(v, seg):
    high = v.astype(BF16)
    low = (v - high.astype(F32)).astype(BF16)
    order = [None] * 4
    order[seg] = high
    order[(seg + 1) % 4] = low
    order[(seg + 2) % 4] = high
    order[(seg + 3) % 4] = jnp.zeros_like(high)
    return jnp.concatenate(order, axis=0)


def invert_blocks(packs):
    shape = packs[0].shape
    row = lax.broadcasted_iota(jnp.int32, shape, 0)
    lane = lax.broadcasted_iota(jnp.int32, shape, 1)
    seg_start = (lane // NB) * NB
    within = lane % NB
    group = 8
    for start in range(0, NB, group):
        columns = [
            [
                jnp.take_along_axis(p, seg_start + (start + q), axis=1, mode="promise_in_bounds")
                for q in range(group)
            ]
            for p in packs
        ]
        for q in range(group):
            j = start + q
            at_row = row == j
            at_lane = within == j
            fresh = []
            for g, p in enumerate(packs):
                cols = columns[g]
                column = cols[q]
                inv = 1.0 / column[j : j + 1, :]
                others = jnp.where(at_row, 0.0, column)
                p = jnp.where(at_lane, jnp.where(at_row, 1.0, 0.0), p)
                scaled = p[j : j + 1, :] * inv
                fresh.append(jnp.where(at_row, scaled, p - others * scaled))
                for r in range(q + 1, group):
                    line = cols[r][j : j + 1, :] * inv
                    cols[r] = jnp.where(at_row, line, cols[r] - others * line)
            packs = fresh
    return packs


def solve_kernel(idx_ref, wt_ref, cnt_ref, prod, o_ref, mat, inv_ref, panels):
    sub = lax.broadcasted_iota(jnp.int32, (176, BS), 0)
    lane = lax.broadcasted_iota(jnp.int32, (176, BS), 1)
    eye_a = jnp.where(sub == lane, K - 1.0, 0.0)
    eye_b = jnp.where((sub == lane + BS) & (sub < K), K - 1.0, 0.0)

    def gather(s, _):
        def add(n, carry):
            b = idx_ref[s, n]
            t = wt_ref[s, n]
            a, rest = carry
            a = a + t * prod[b, :, pl.ds(0, BS)].astype(F32)
            rest = rest + t * prod[b, :, pl.ds(BS, BS)].astype(F32)
            return a, rest

        a, rest = lax.fori_loop(0, cnt_ref[s], add, (eye_a, eye_b))
        live = lane[:K] < NB
        mat[s, pl.ds(0, K), pl.ds(0, BS)] = a[:K]
        mat[s, pl.ds(0, K), pl.ds(BS, BS)] = jnp.where(live, rest[:K], 0.0)
        ra = jnp.sum(a[K : K + 8], axis=0, keepdims=True)
        rb = jnp.sum(jnp.where(live[:8], rest[K : K + 8], 0.0), axis=0, keepdims=True)
        mat[s, pl.ds(K, 8), pl.ds(0, BS)] = jnp.broadcast_to(ra, (8, BS))
        mat[s, pl.ds(K, 8), pl.ds(BS, BS)] = jnp.broadcast_to(rb, (8, BS))
        return 0

    lax.fori_loop(0, 16, gather, 0)

    lane_b = lax.broadcasted_iota(jnp.int32, (NB, BS), 1)
    sub_b = lax.broadcasted_iota(jnp.int32, (NB, BS), 0)
    lane_f = lax.broadcasted_iota(jnp.int32, (K + 8, BS), 1)
    for k in range(K // NB):
        tile, seg = (k * NB) // BS, k % 4
        packs = []
        for g in range(4):
            pack = jnp.zeros((NB, BS), F32)
            for q in range(4):
                block = mat[4 * g + q, pl.ds(k * NB, NB), pl.ds(tile * BS, BS)]
                if q != seg:
                    block = pltpu.roll(block, ((q - seg) * NB) % BS, 1)
                pack = jnp.where(lane_b // NB == q, block, pack)
            packs.append(pack)
        packs = invert_blocks(packs)
        for g in range(4):
            for q in range(4):
                inv_ref[4 * g + q] = left_parts(packs[g], q)

        at_seg = lane_b // NB == seg
        eye_seg = jnp.where(at_seg & (sub_b == lane_b - seg * NB), 1.0, 0.0)

        for s in range(16):
            panel = [mat[s, pl.ds(k * NB, NB), pl.ds(t * BS, BS)] for t in range(2)]
            panel[tile] = jnp.where(at_seg, eye_seg, panel[tile])
            panels[s] = dot(inv_ref[s], right_parts(jnp.concatenate(panel, axis=1), s % 4))
        for s in range(16):
            scaled = panels[s]
            left = left_parts(mat[s, :, pl.ds(tile * BS, BS)], seg)
            taken = dot(left, right_parts(scaled, seg))
            for t in range(2):
                old = mat[s, :, pl.ds(t * BS, BS)]
                if t == tile:
                    old = jnp.where(lane_f // NB == seg, 0.0, old)
                mat[s, :, pl.ds(t * BS, BS)] = old - taken[:, t * BS : (t + 1) * BS]
            mat[s, pl.ds(k * NB, NB), :] = scaled

    half = (K - 1) / 2.0
    diag_a = jnp.where(sub[:K] == lane[:K], 0.5, 0.0)
    diag_b = jnp.where(sub[:K] == lane[:K] + BS, 0.5, 0.0)

    seg40 = lane[:40] // NB
    for s in range(16):
        wa = mat[s, pl.ds(K, 1), pl.ds(0, BS)]
        wb = mat[s, pl.ds(K, 1), pl.ds(BS, BS)]
        ta = diag_a + half * mat[s, pl.ds(0, K), pl.ds(0, BS)] - wa
        tb = diag_b + half * mat[s, pl.ds(0, K), pl.ds(BS, BS)] - wb
        folded = tb[:40]
        for g in range(1, 4):
            folded = jnp.where(seg40 == g, pltpu.roll(tb[40 * g : 40 * g + 40], NB * g, 1), folded)
        o_ref[s % 2, s // 2, pl.ds(0, K), :] = ta.astype(BF16)
        folded = jnp.concatenate([folded, jnp.zeros((8, BS), F32)], axis=0)
        o_ref[s % 2, s // 2, pl.ds(K, 48), :] = folded.astype(BF16)


def solve(indices, tapers, totals, products):
    vmem = pl.BlockSpec(memory_space=pltpu.VMEM)
    smem = pl.BlockSpec(memory_space=pltpu.SMEM)
    return pl.pallas_call(
        solve_kernel,
        out_shape=jax.ShapeDtypeStruct((2, 8, TROWS, BS), BF16),
        in_specs=[smem, smem, smem, vmem],
        out_specs=vmem,
        scratch_shapes=[
            pltpu.VMEM((16, K + 8, 2 * BS), F32),
            pltpu.VMEM((16, NB, BS), BF16),
            pltpu.VMEM((16, NB, 2 * BS), F32),
        ],
        compiler_params=params(),
        name="solve",
    )(indices, tapers, totals, products.reshape(64, WROWS, 2 * BS))


def pair_lists(pattern):
    x, y, core = position()
    own = lax.dynamic_index_in_dim(pattern, level_at(x, y), 1, keepdims=False)
    home = jnp.arange(16, dtype=jnp.int32) // 2
    index = index_of(x + (home // 4) * toward(x, y), home, core)
    columns = index * 2 + jnp.arange(16, dtype=jnp.int32) % 2
    batches = jnp.arange(64, dtype=jnp.int32)
    matches = jnp.sum((own[None] == columns[:, None, None]).astype(F32), axis=2)
    spacing = jnp.abs(columns[:, None] - batches[None, :])
    spacing = jnp.minimum(spacing, 64 - spacing).astype(F32)
    radius = 2.0 * spacing / 64
    weight = (
        ((-0.25 * radius + 0.5) * radius + 0.625) * radius - 5.0 / 3.0
    ) * radius * radius + 1.0
    taper = lax.reduce_precision(matches * weight, 8, 7)
    away = ((batches // 2) % 2 != core).astype(jnp.int32)
    slots = (batches % 2) * 32 + away * 16 + batches // 4
    upto = (batches[:, None] <= batches[None, :]).astype(F32)
    place = jnp.sum(matches[:, :, None] * upto[None], axis=1) - 1.0
    chosen = (place[:, None, :] == batches[None, :, None].astype(F32)) * matches[:, None, :]
    indices = jnp.sum(chosen * slots.astype(F32), axis=2).astype(jnp.int32)
    tapers = jnp.sum(chosen * taper[:, None, :], axis=2)
    totals = jnp.sum(matches, axis=1).astype(jnp.int32)
    return indices, tapers, totals


def per_device(ensemble, obs_values, obs_var, obs_cols, obs_counts, pattern):
    indices, tapers, totals = pair_lists(pattern)
    products, anomalies, means = forward(ensemble, obs_values, obs_var, obs_cols, obs_counts)
    analysed = back(solve(indices, tapers, totals, products), anomalies, means)
    result = jnp.transpose(analysed.reshape(2, NZ, MZ, 8, BS), (2, 0, 1, 3, 4))
    return result.reshape(MZ, 2, 64, BS)


def solution(mesh):
    placed = (
        P("mem", "dom", None, None),
        P("dom", "mem", None),
        P("dom", "mem", None),
        P("dom", "mem", None),
        P("dom", "mem"),
        P(None, "mem", None),
    )
    return jax.shard_map(
        per_device,
        mesh=mesh,
        in_specs=placed,
        out_specs=P("mem", "dom", None, None),
        check_vma=False,
    )
```

```python
import jax
import jax.numpy as jnp
from jax import lax
from jax.experimental import pallas as pl
from jax.experimental.pallas import tpu as pltpu
from jax.sharding import PartitionSpec as P

F32 = jnp.float32
BF16 = jnp.bfloat16
MESH = pl.DeviceIdType.MESH

K = 160
BS = 128
NZ = 8
MZ = 20
ROWS = 160
WROWS = 176
TROWS = 208
NB = 32
VMEM_LIMIT = 48 * 1024 * 1024
VMEM_FORWARD = 63 * 1024 * 1024


def params(limit=VMEM_LIMIT, **more):
    return pltpu.CompilerParams(vmem_limit_bytes=limit, **more)


def dot(a, b):
    return jnp.dot(a, b, preferred_element_type=F32)


def position():
    me = lax.axis_index("dom")
    return me // 8, lax.rem(me // 2, 4), lax.rem(me, 2)


def index_of(x, y, core):
    return lax.rem(x + 8, 4) * 8 + lax.rem(y + 8, 4) * 2 + core


def toward(x, y):
    return 2 * lax.rem(x + y + 8, 2) - 1


def level_at(x, y):
    x, y = lax.rem(x + 8, 4), lax.rem(y + 8, 4)
    return y * 2 + lax.rem(x + 3 * lax.rem(y, 2), 4) // 2


NEAR = [(k, dy) for dy in (0, 1, 3, 2) for k in (0, 1)]


def signal_dom(sem, index):
    pl.semaphore_signal(sem, inc=1, device_id={"dom": index}, device_id_type=MESH)


def push(src, dst, send_sem, recv_sem, **to):
    copy = pltpu.make_async_remote_copy(
        src_ref=src,
        dst_ref=dst,
        send_sem=send_sem,
        recv_sem=recv_sem,
        device_id=to,
        device_id_type=MESH,
    )
    copy.start()
    return copy


def stay(src, dst, sem):
    copy = pltpu.make_async_copy(src, dst, sem)
    copy.start()
    return copy


def observe_column(c, e_ref, val_ref, var_ref, col_ref, cnt_ref, w_ref, a_ref, m_ref, wide):
    for z in range(NZ):
        wide[pl.ds(z * ROWS, ROWS), :] = e_ref[c, z].astype(F32)
    sub = lax.broadcasted_iota(jnp.int32, (BS, BS), 0)
    lane = lax.broadcasted_iota(jnp.int32, (1, BS), 1)
    row16 = lax.broadcasted_iota(jnp.int32, (16, BS), 0)
    for l in range(8):
        cl = c * 8 + l
        states = wide[pl.ds(l, K, stride=8), :]
        mean = jnp.sum(states, axis=0, keepdims=True) / K
        anom = (states - mean).astype(BF16)
        a_ref[cl] = anom
        m_ref[pl.ds(cl, 1), :] = mean
        high = mean.astype(BF16)
        rest = mean - high.astype(F32)
        mid = rest.astype(BF16)
        low = (rest - mid.astype(F32)).astype(BF16)
        parts = jnp.where(
            row16 == 0,
            high.astype(F32),
            jnp.where(row16 == 1, mid.astype(F32), jnp.where(row16 == 2, low.astype(F32), 0.0)),
        ).astype(BF16)
        picked = (sub == col_ref[c, pl.ds(l, 1), :]).astype(F32).astype(BF16)
        seen = dot(jnp.concatenate([anom, parts], axis=0), picked)
        live = (lane < cnt_ref[c, l]).astype(F32)
        spread = jnp.sqrt(var_ref[c, pl.ds(l, 1), :])
        w_ref[c, l, pl.ds(0, K), :] = (seen[:K] * (live / spread)).astype(BF16)
        mean_seen = seen[K : K + 1] + seen[K + 1 : K + 2] + seen[K + 2 : K + 3]
        resid = live * (val_ref[c, pl.ds(l, 1), :] - mean_seen) / spread
        w_ref[c, l, pl.ds(K, 16), :] = jnp.where(row16 == 0, resid, 0.0).astype(BF16)


class Swap:
    def __init__(self, source, target, send_sem, recv_sem, own_sem):
        z = lax.axis_index("mem")
        self.own = (source.at[z], target.at[z], own_sem)
        self.parts = []
        for i in (4, 5, 3, 6, 2, 7, 1):
            to = lax.rem(z + i, NZ)
            self.parts.append((source.at[to], target.at[z], send_sem.at[i], recv_sem.at[i], to))

    def begin(self):
        self.copies = [push(*part, mem=to) for *part, to in self.parts]
        self.own = stay(*self.own)

    def arrive(self):
        for copy in self.copies:
            copy.wait_recv()
        self.own.wait()

    def finish(self):
        for copy in self.copies:
            copy.wait_send()


def greet_mem(barrier):
    z = lax.axis_index("mem")
    for i in range(1, NZ):
        pl.semaphore_signal(
            barrier, inc=1, device_id={"mem": lax.rem(z + i, NZ)}, device_id_type=MESH
        )


def forward_kernel(
    ens_ref, val_ref, var_ref, col_ref, cnt_ref,
    prod_ref, a_ref, m_ref,
    ens, val_buf, var_buf, col_buf, x_buf, e_buf, wide, a_buf, m_buf, w_buf, wall, prod,
    z_send, z_recv, n_send, n_recv, f_send, f_recv, p_send, p_recv, own_sem, out_sem, in_sem,
):
    me = lax.axis_index("dom")
    x, y, core = position()
    e = toward(x, y)
    partner = index_of(x - e, y, core)
    sibling = index_of(x, y, 1 - core)
    mine = level_at(x, y)

    load = stay(ens_ref, ens, in_sem.at[0])
    loads = [
        stay(val_ref, val_buf, in_sem.at[1]),
        stay(var_ref, var_buf, in_sem.at[2]),
        stay(col_ref, col_buf, in_sem.at[3]),
    ]
    barrier = pltpu.get_barrier_semaphore()
    greet_mem(barrier)
    for k, dy in NEAR[1:]:
        signal_dom(barrier, index_of(x + k * e, y - dy, core))
    signal_dom(barrier, partner)
    signal_dom(barrier, sibling)

    def regroup(c):
        for j in range(NZ // 2):
            rows = ens[:, c, pl.ds(16 * j, 16), :].astype(F32)
            for half in range(2):
                part = rows[:, 8 * half : 8 * half + 8].reshape(ROWS, BS)
                x_buf[c, 2 * j + half] = part.astype(BF16)

    direct, relayed, paired, owns = [{}, {}], [{}, {}], [{}, {}], []

    def to_sibling(c, n, src, slot):
        paired[c][n] = push(
            src, wall.at[c, slot], p_send.at[c, n], p_recv.at[c, n], dom=sibling
        )

    def to_partner(c, n, src, slot):
        relayed[c][n] = push(
            src, wall.at[c, slot], f_send.at[c, n], f_recv.at[c, n], dom=partner
        )

    def send_near(c):
        for k, dy in reversed(NEAR[1:]):
            tx, ty = x + k * toward(x, y + dy), y + dy
            direct[c][k, dy] = push(
                w_buf.at[c, level_at(tx, ty)],
                wall.at[c, me],
                n_send.at[c, k * 4 + dy],
                n_recv.at[c, k * 4 + dy],
                dom=index_of(tx, ty, core),
            )
        source = w_buf.at[c, mine]
        to_partner(c, 0, source, me)
        to_sibling(c, 0, source, me)
        owns.append(stay(source, wall.at[c, me], own_sem.at[2 + c]))

    def from_near(c, k, dy):
        direct[c][k, dy].wait_recv()
        slot = index_of(x + k * e, y - dy, core)
        to_partner(c, k * 4 + dy, wall.at[c, slot], slot)
        to_sibling(c, k * 4 + dy, wall.at[c, slot], slot)

    def from_partner(c, k, dy):
        relayed[c][k * 4 + dy].wait_recv()
        slot = index_of(x - e - k * e, y - dy, core)
        to_sibling(c, 8 + k * 4 + dy, wall.at[c, slot], slot)

    def multiply(c, which, n):
        slot = 2 * n + (core if which == 0 else 1 - core)
        full = lax.dot_general(
            wall[c, slot], wall[c, slot, pl.ds(0, K), :],
            (((1,), (1,)), ((), ())),
            preferred_element_type=F32,
        )
        full = jnp.concatenate([full, jnp.zeros((WROWS, 2 * BS - K), F32)], axis=1)
        prod[c, which, n] = full.astype(BF16)

    def near_slot(k, dy):
        return index_of(x + k * e, y - dy, core) // 2

    def far_slot(k, dy):
        return index_of(x - e - k * e, y - dy, core) // 2

    def multiply_group(c, which, slot):
        def body(n, _):
            multiply(c, which, slot(n // 4, lax.rem(n, 4)))
            return 0

        lax.fori_loop(0, 8, body, 0, unroll=4)

    outs = []

    def write(c, which):
        n = c * 2 + which
        outs.append(stay(prod.at[c, which], prod_ref.at[c, which], out_sem.at[n]))

    swaps = [
        Swap(
            x_buf.at[c], e_buf.at[c], z_send.at[c], z_recv.at[c], own_sem.at[c]
        )
        for c in range(2)
    ]

    def observe(c):
        observe_column(
            c, e_buf, val_buf, var_buf, col_buf, cnt_ref, w_buf, a_buf, m_buf, wide
        )
        send_near(c)

    def multiply_paired(c, slot, first):
        for n in range(first, first + 8):
            paired[c][n].wait_recv()
        multiply_group(c, 1, slot)

    load.wait()
    regroup(0)
    pl.semaphore_wait(barrier, NZ - 1 + 9)
    swaps[0].begin()
    regroup(1)
    swaps[0].finish()
    swaps[1].begin()
    for copy in loads:
        copy.wait()
    swaps[0].arrive()
    observe(0)
    for k, dy in NEAR[1:]:
        from_near(0, k, dy)
    owns[0].wait()
    multiply_group(0, 0, near_slot)
    swaps[1].arrive()
    observe(1)
    outs.append(stay(a_buf, a_ref, out_sem.at[4]))
    outs.append(stay(m_buf, m_ref, out_sem.at[5]))
    for k, dy in NEAR:
        from_partner(0, k, dy)
        multiply(0, 0, far_slot(k, dy))
    write(0, 0)
    owns[1].wait()
    for n in range(8):
        paired[0][n].wait_recv()
    for n, (k, dy) in enumerate(NEAR):
        if n:
            from_near(1, k, dy)
        multiply(0, 1, near_slot(k, dy))
    for n in range(8, 16):
        paired[0][n].wait_recv()
    for k, dy in NEAR:
        from_partner(1, k, dy)
        multiply(0, 1, far_slot(k, dy))
        multiply(1, 0, near_slot(k, dy))
    write(0, 1)
    multiply_group(1, 0, far_slot)
    write(1, 0)
    multiply_paired(1, near_slot, 0)
    multiply_paired(1, far_slot, 8)
    write(1, 1)
    swaps[1].finish()
    for c in range(2):
        for group in (direct[c], relayed[c], paired[c]):
            for copy in group.values():
                copy.wait_send()
    for copy in outs:
        copy.wait()


def forward(x, values, variances, columns, counts):
    hbm = pl.BlockSpec(memory_space=pltpu.HBM)
    dma = pltpu.SemaphoreType.DMA
    return pl.pallas_call(
        forward_kernel,
        out_shape=(
            jax.ShapeDtypeStruct((2, 2, 16, WROWS, 2 * BS), BF16),
            jax.ShapeDtypeStruct((16, K, BS), BF16),
            jax.ShapeDtypeStruct((16, BS), F32),
        ),
        in_specs=[hbm] * 4 + [pl.BlockSpec(memory_space=pltpu.SMEM)],
        out_specs=(hbm, hbm, hbm),
        scratch_shapes=[
            pltpu.VMEM((MZ, 2, 64, BS), BF16),
            pltpu.VMEM((2, 8, BS), F32),
            pltpu.VMEM((2, 8, BS), F32),
            pltpu.VMEM((2, 8, BS), jnp.int32),
            pltpu.VMEM((2, NZ, ROWS, BS), BF16),
            pltpu.VMEM((2, NZ, ROWS, BS), BF16),
            pltpu.VMEM((NZ * ROWS, BS), F32),
            pltpu.VMEM((16, K, BS), BF16),
            pltpu.VMEM((16, BS), F32),
            pltpu.VMEM((2, 8, WROWS, BS), BF16),
            pltpu.VMEM((2, 32, WROWS, BS), BF16),
            pltpu.VMEM((2, 2, 16, WROWS, 2 * BS), BF16),
            dma((2, 9)), dma((2, 9)), dma((2, 8)), dma((2, 8)), dma((2, 8)), dma((2, 8)),
            dma((2, 16)), dma((2, 16)), dma((4,)), dma((6,)), dma((4,)),
        ],
        compiler_params=params(VMEM_FORWARD, collective_id=0, has_side_effects=True),
        name="forward",
    )(x, values, variances, columns, counts)


def back_kernel(
    t_ref, a_ref, m_ref, o_ref,
    t_buf, a_buf, m_buf, wide, out_buf,
    n_send, n_recv, z_send, z_recv, own_sem, in_sem,
):
    x, y, core = position()
    e = toward(x, y)
    mine = level_at(x, y)

    barrier = pltpu.get_barrier_semaphore()
    greet_mem(barrier)
    for k, dy in NEAR[1:]:
        signal_dom(barrier, index_of(x + k * toward(x, y - dy), y - dy, core))
    pl.semaphore_wait(barrier, NZ - 1 + 7)

    loads = [stay(a_ref, a_buf, in_sem.at[0]), stay(m_ref, m_buf, in_sem.at[1])]
    returns, owns = [], []

    def give(c):
        returns.append([])
        for k, dy in reversed(NEAR[1:]):
            n = k * 4 + dy
            returns[c].append(
                push(
                    t_ref.at[c, k * 4 + lax.rem(y + dy, 4)],
                    t_buf.at[c, mine],
                    n_send.at[c, n],
                    n_recv.at[c, n],
                    dom=index_of(x + k * e, y + dy, core),
                )
            )
        owns.append(stay(t_ref.at[c, y], t_buf.at[c, mine], own_sem.at[c]))

    none = jnp.zeros((BS - NB, BS), BF16)

    def apply(c):
        for l in range(8):
            anom = a_buf[c * 8 + l]
            folded = t_buf[c, l, pl.ds(K, 48), :].astype(F32)[:40]
            opened = [folded] + [pltpu.roll(folded, BS - NB * g, 1) for g in range(1, 4)]
            rest = jnp.concatenate(opened, axis=0).astype(BF16)
            left = jnp.concatenate([t_buf[c, l, pl.ds(0, K), :], rest], axis=1)
            right = jnp.concatenate([anom, none], axis=0)
            wide[pl.ds(l, K, stride=8), :] = m_buf[pl.ds(c * 8 + l, 1), :] + dot(left, right)
        for g in range(NZ):
            out_buf[c, g] = wide[pl.ds(g * ROWS, ROWS), :].astype(BF16)

    swaps = [
        Swap(
            out_buf.at[c], o_ref.at[c], z_send.at[c], z_recv.at[c], own_sem.at[2 + c]
        )
        for c in range(2)
    ]
    give(0)
    for copy in returns[0]:
        copy.wait_send()
    give(1)
    for copy in loads:
        copy.wait()
    for c in range(2):
        for copy in returns[c]:
            copy.wait_recv()
        owns[c].wait()
        apply(c)
        swaps[c].begin()
    for copy in returns[1]:
        copy.wait_send()
    for swap in swaps:
        swap.arrive()
        swap.finish()


def back(t, anomalies, means):
    hbm = pl.BlockSpec(memory_space=pltpu.HBM)
    dma = pltpu.SemaphoreType.DMA
    return pl.pallas_call(
        back_kernel,
        out_shape=jax.ShapeDtypeStruct((2, NZ, ROWS, BS), BF16),
        in_specs=[hbm, hbm, hbm],
        out_specs=hbm,
        scratch_shapes=[
            pltpu.VMEM((2, 8, TROWS, BS), BF16),
            pltpu.VMEM((16, K, BS), BF16),
            pltpu.VMEM((16, BS), F32),
            pltpu.VMEM((NZ * ROWS, BS), F32),
            pltpu.VMEM((2, NZ, ROWS, BS), BF16),
            dma((2, 8)), dma((2, 8)), dma((2, 9)), dma((2, 9)), dma((4,)), dma((2,)),
        ],
        compiler_params=params(collective_id=1, has_side_effects=True),
        name="back",
    )(t, anomalies, means)


def left_parts(v, seg):
    lane = lax.broadcasted_iota(jnp.int32, v.shape, 1) // NB
    high = v.astype(BF16).astype(F32)
    low = v - high
    out = jnp.where(lane == seg, high, 0.0)
    out = jnp.where(lane == (seg + 1) % 4, pltpu.roll(high, NB, 1), out)
    out = jnp.where(lane == (seg + 2) % 4, pltpu.roll(low, 2 * NB, 1), out)
    return out.astype(BF16)


def right_parts(v, seg):
    high = v.astype(BF16)
    low = (v - high.astype(F32)).astype(BF16)
    order = [None] * 4
    order[seg] = high
    order[(seg + 1) % 4] = low
    order[(seg + 2) % 4] = high
    order[(seg + 3) % 4] = jnp.zeros_like(high)
    return jnp.concatenate(order, axis=0)


def invert_blocks(packs):
    shape = packs[0].shape
    row = lax.broadcasted_iota(jnp.int32, shape, 0)
    lane = lax.broadcasted_iota(jnp.int32, shape, 1)
    seg_start = (lane // NB) * NB
    within = lane % NB
    group = 8
    for start in range(0, NB, group):
        columns = [
            [
                jnp.take_along_axis(p, seg_start + (start + q), axis=1, mode="promise_in_bounds")
                for q in range(group)
            ]
            for p in packs
        ]
        for q in range(group):
            j = start + q
            at_row = row == j
            at_lane = within == j
            fresh = []
            for g, p in enumerate(packs):
                cols = columns[g]
                column = cols[q]
                inv = 1.0 / column[j : j + 1, :]
                others = jnp.where(at_row, 0.0, column)
                p = jnp.where(at_lane, jnp.where(at_row, 1.0, 0.0), p)
                scaled = p[j : j + 1, :] * inv
                fresh.append(jnp.where(at_row, scaled, p - others * scaled))
                for r in range(q + 1, group):
                    line = cols[r][j : j + 1, :] * inv
                    cols[r] = jnp.where(at_row, line, cols[r] - others * line)
            packs = fresh
    return packs


def solve_kernel(idx_ref, wt_ref, cnt_ref, prod, o_ref, mat, inv_ref, panels):
    sub = lax.broadcasted_iota(jnp.int32, (176, BS), 0)
    lane = lax.broadcasted_iota(jnp.int32, (176, BS), 1)
    eye_a = jnp.where(sub == lane, K - 1.0, 0.0)
    eye_b = jnp.where((sub == lane + BS) & (sub < K), K - 1.0, 0.0)

    def gather(s, _):
        def add(n, carry):
            b = idx_ref[s, n]
            t = wt_ref[s, n]
            a, rest = carry
            a = a + t * prod[b, :, pl.ds(0, BS)].astype(F32)
            rest = rest + t * prod[b, :, pl.ds(BS, BS)].astype(F32)
            return a, rest

        a, rest = lax.fori_loop(0, cnt_ref[s], add, (eye_a, eye_b))
        live = lane[:K] < NB
        mat[s, pl.ds(0, K), pl.ds(0, BS)] = a[:K]
        mat[s, pl.ds(0, K), pl.ds(BS, BS)] = jnp.where(live, rest[:K], 0.0)
        ra = jnp.sum(a[K : K + 8], axis=0, keepdims=True)
        rb = jnp.sum(jnp.where(live[:8], rest[K : K + 8], 0.0), axis=0, keepdims=True)
        mat[s, pl.ds(K, 8), pl.ds(0, BS)] = jnp.broadcast_to(ra, (8, BS))
        mat[s, pl.ds(K, 8), pl.ds(BS, BS)] = jnp.broadcast_to(rb, (8, BS))
        return 0

    lax.fori_loop(0, 16, gather, 0)

    lane_b = lax.broadcasted_iota(jnp.int32, (NB, BS), 1)
    sub_b = lax.broadcasted_iota(jnp.int32, (NB, BS), 0)
    lane_f = lax.broadcasted_iota(jnp.int32, (K + 8, BS), 1)
    for k in range(K // NB):
        tile, seg = (k * NB) // BS, k % 4
        packs = []
        for g in range(4):
            pack = jnp.zeros((NB, BS), F32)
            for q in range(4):
                block = mat[4 * g + q, pl.ds(k * NB, NB), pl.ds(tile * BS, BS)]
                if q != seg:
                    block = pltpu.roll(block, ((q - seg) * NB) % BS, 1)
                pack = jnp.where(lane_b // NB == q, block, pack)
            packs.append(pack)
        packs = invert_blocks(packs)
        for g in range(4):
            for q in range(4):
                inv_ref[4 * g + q] = left_parts(packs[g], q)

        at_seg = lane_b // NB == seg
        eye_seg = jnp.where(at_seg & (sub_b == lane_b - seg * NB), 1.0, 0.0)

        for s in range(16):
            panel = [mat[s, pl.ds(k * NB, NB), pl.ds(t * BS, BS)] for t in range(2)]
            panel[tile] = jnp.where(at_seg, eye_seg, panel[tile])
            panels[s] = dot(inv_ref[s], right_parts(jnp.concatenate(panel, axis=1), s % 4))
        for s in range(16):
            scaled = panels[s]
            left = left_parts(mat[s, :, pl.ds(tile * BS, BS)], seg)
            taken = dot(left, right_parts(scaled, seg))
            for t in range(2):
                old = mat[s, :, pl.ds(t * BS, BS)]
                if t == tile:
                    old = jnp.where(lane_f // NB == seg, 0.0, old)
                mat[s, :, pl.ds(t * BS, BS)] = old - taken[:, t * BS : (t + 1) * BS]
            mat[s, pl.ds(k * NB, NB), :] = scaled

    half = (K - 1) / 2.0
    diag_a = jnp.where(sub[:K] == lane[:K], 0.5, 0.0)
    diag_b = jnp.where(sub[:K] == lane[:K] + BS, 0.5, 0.0)

    seg40 = lane[:40] // NB
    for s in range(16):
        wa = mat[s, pl.ds(K, 1), pl.ds(0, BS)]
        wb = mat[s, pl.ds(K, 1), pl.ds(BS, BS)]
        ta = diag_a + half * mat[s, pl.ds(0, K), pl.ds(0, BS)] - wa
        tb = diag_b + half * mat[s, pl.ds(0, K), pl.ds(BS, BS)] - wb
        folded = tb[:40]
        for g in range(1, 4):
            folded = jnp.where(seg40 == g, pltpu.roll(tb[40 * g : 40 * g + 40], NB * g, 1), folded)
        o_ref[s % 2, s // 2, pl.ds(0, K), :] = ta.astype(BF16)
        folded = jnp.concatenate([folded, jnp.zeros((8, BS), F32)], axis=0)
        o_ref[s % 2, s // 2, pl.ds(K, 48), :] = folded.astype(BF16)


def solve(indices, tapers, totals, products):
    vmem = pl.BlockSpec(memory_space=pltpu.VMEM)
    smem = pl.BlockSpec(memory_space=pltpu.SMEM)
    return pl.pallas_call(
        solve_kernel,
        out_shape=jax.ShapeDtypeStruct((2, 8, TROWS, BS), BF16),
        in_specs=[smem, smem, smem, vmem],
        out_specs=vmem,
        scratch_shapes=[
            pltpu.VMEM((16, K + 8, 2 * BS), F32),
            pltpu.VMEM((16, NB, BS), BF16),
            pltpu.VMEM((16, NB, 2 * BS), F32),
        ],
        compiler_params=params(),
        name="solve",
    )(indices, tapers, totals, products.reshape(64, WROWS, 2 * BS))


def pair_lists(pattern):
    x, y, core = position()
    own = lax.dynamic_index_in_dim(pattern, level_at(x, y), 1, keepdims=False)
    home = jnp.arange(16, dtype=jnp.int32) // 2
    index = index_of(x + (home // 4) * toward(x, y), home, core)
    columns = index * 2 + jnp.arange(16, dtype=jnp.int32) % 2
    batches = jnp.arange(64, dtype=jnp.int32)
    matches = jnp.sum((own[None] == columns[:, None, None]).astype(F32), axis=2)
    spacing = jnp.abs(columns[:, None] - batches[None, :])
    spacing = jnp.minimum(spacing, 64 - spacing).astype(F32)
    radius = 2.0 * spacing / 64
    weight = (
        ((-0.25 * radius + 0.5) * radius + 0.625) * radius - 5.0 / 3.0
    ) * radius * radius + 1.0
    taper = lax.reduce_precision(matches * weight, 8, 7)
    away = ((batches // 2) % 2 != core).astype(jnp.int32)
    slots = (batches % 2) * 32 + away * 16 + batches // 4
    upto = (batches[:, None] <= batches[None, :]).astype(F32)
    place = jnp.sum(matches[:, :, None] * upto[None], axis=1) - 1.0
    chosen = (place[:, None, :] == batches[None, :, None].astype(F32)) * matches[:, None, :]
    indices = jnp.sum(chosen * slots.astype(F32), axis=2).astype(jnp.int32)
    tapers = jnp.sum(chosen * taper[:, None, :], axis=2)
    totals = jnp.sum(matches, axis=1).astype(jnp.int32)
    return indices, tapers, totals


def per_device(ensemble, obs_values, obs_var, obs_cols, obs_counts, pattern):
    indices, tapers, totals = pair_lists(pattern)
    products, anomalies, means = forward(ensemble, obs_values, obs_var, obs_cols, obs_counts)
    analysed = back(solve(indices, tapers, totals, products), anomalies, means)
    result = jnp.transpose(analysed.reshape(2, NZ, MZ, 8, BS), (2, 0, 1, 3, 4))
    return result.reshape(MZ, 2, 64, BS)


def solution(mesh):
    placed = (
        P("mem", "dom", None, None),
        P("dom", "mem", None),
        P("dom", "mem", None),
        P("dom", "mem", None),
        P("dom", "mem"),
        P(None, "mem", None),
    )
    return jax.shard_map(
        per_device,
        mesh=mesh,
        in_specs=placed,
        out_specs=P("mem", "dom", None, None),
        check_vma=False,
    )
```
